32 devices in a mesh: gx: 8 (over z, core), gy: 4 (over y, x).
Axes of the slice: x: 2, y: 2, z: 4, core: 2. Of those that a mesh axis runs over, the one named last changes fastest.
Arguments:
- probes: bfloat16 [8, 262144], P(None, ('gx', 'gy')), may hold values from -6 to 6
- cells: int32 [3, 262144], P(None, ('gx', 'gy')), may hold values from 0 to 1023, as said below
- fractions: float32 [3, 262144], P(None, ('gx', 'gy')), may hold values from 0 to 1
- counts: int32 [8, 4], P('gx', 'gy'), may hold values from 0 to 64, as said below
- kx: bfloat16 [1024, 1024], P('gx'), may hold values from 0 to 1
- ky: bfloat16 [1024, 1024], P('gy'), may hold values from 0 to 1
- kt: float32 [4, 4], replicated, may hold values from 0.25 to 1
Outputs:
- applied: bfloat16 [8, 262144], P(None, ('gx', 'gy'))
The draws below stay inside these ranges and needn't reach their ends.
Inputs may be any that keep to these rules, and one draw needn't show every extreme that they name: cells[0] lies in the x rows 128 * i to 128 * i + 127 and cells[1] in the y columns 256 * j to 256 * j + 255, where the slot lies on the device at index i of gx and j of gy; cells[2] is below 3. `counts`: slots of blocks at or past a device's count hold no observation; some device has 64 live blocks.
All inputs are finite; a program needn't handle non-finite values.
Results may differ from the reference program's by a relative error of at most 0.002.
The reference program's roundings to bfloat16 on the way count: a program that leaves them out, or rounds other values in their place, can miss the bound.
Values may be sent and summed in bfloat16 or wider, within the bound.
A program may use at most 64 MiB of HBM per device.

```python
import jax
import jax.numpy as jnp
from jax import lax

NX = 1024
NY = 1024
DAYS = 4
PROBES = 8
BLOCK = 128
BLK_DEV = 64
PTS_DEV = 8192
NPTS = 262144
TILES_X = 8
TILES_Y = 4
CX = 128
CY = 256
ELL_X = 512
ELL_Y = 512


def draw_cells(key, part):
    slots = jnp.arange(NPTS, dtype=jnp.int32)
    device = slots // PTS_DEV
    tile_x = device // TILES_Y
    tile_y = device % TILES_Y
    row_cell = tile_x * CX + jax.random.randint(jax.random.fold_in(key, 1), (NPTS,), 0, CX)
    col_cell = tile_y * CY + jax.random.randint(jax.random.fold_in(key, 2), (NPTS,), 0, CY)
    day_cell = jax.random.randint(jax.random.fold_in(key, 3), (NPTS,), 0, DAYS - 1)
    return jnp.stack([row_cell, col_cell, day_cell]).astype(jnp.int32)


def draw_counts(key, part):
    tiles = TILES_X * TILES_Y
    drawn_root = jax.random.randint(jax.random.fold_in(key, 11), (tiles,), 0, BLK_DEV + 1)
    loads = drawn_root * drawn_root // BLK_DEV
    fullest = jax.random.randint(jax.random.fold_in(key, 12), (), 0, tiles)
    loads = jnp.where(jnp.arange(tiles, dtype=jnp.int32) == fullest, BLK_DEV, loads)
    return loads.reshape(TILES_X, TILES_Y).astype(jnp.int32)


def kernel_factor(key, order, reach_cells, roughness):
    position = jnp.arange(order, dtype=jnp.float32)
    distance = jnp.abs(position[:, None] - position[None, :])
    return jnp.exp(-distance / reach_cells) * roughness / jnp.sqrt(jnp.float32(reach_cells))


def draw_kx(key, part):
    roughness = jax.random.uniform(jax.random.fold_in(key, 21), (NX, NX), jnp.float32, 0.5, 1.5)
    return kernel_factor(key, NX, ELL_X, roughness).astype(jnp.bfloat16)


def draw_ky(key, part):
    roughness = jax.random.uniform(jax.random.fold_in(key, 31), (NY, NY), jnp.float32, 0.5, 1.5)
    return kernel_factor(key, NY, ELL_Y, roughness).astype(jnp.bfloat16)


def levels(key, dims, shards, low, top_value):
    def one(dim, blocks):
        heights = jax.random.uniform(jax.random.fold_in(jax.random.fold_in(key, 6), dim), (blocks,), jnp.float32, low / len(shards), top_value / len(shards))
        return jnp.repeat(jnp.exp(heights), dims[dim] // blocks).reshape((-1,) + (1,) * (len(dims) - dim - 1))

    level = one(*shards[0])
    for cut in shards[1:]:
        level = level * one(*cut)
    return level


def scatter_about(own_key, shape, scale, bound, pieces=(), kind=jnp.bfloat16):
    array = jax.random.normal(own_key, shape, jnp.float32) * scale
    if len(pieces) > 0:
        array = levels(own_key, shape, pieces, -0.22, 0.18) * array
    return jnp.clip(array, min=-bound, max=bound).astype(kind)


def setup_inputs(seed: int = 0) -> dict:
    key_list = jax.random.split(jax.random.key(seed), 8)
    probes = scatter_about(key_list[0], (PROBES, NPTS), 1.0, 6.0, ((1, 32),))
    cells = draw_cells(jax.random.fold_in(key_list[7], 71), 0)
    fractions = jnp.clip(1.0 * jax.random.uniform(key_list[2], (3, NPTS), jnp.float32) ** levels(key_list[2], (3, NPTS), ((1, 32),), -0.2, 0.2), 0.0, 1.0)
    counts = draw_counts(jax.random.fold_in(key_list[7], 71), 0)
    kx = draw_kx(jax.random.fold_in(key_list[7], 71), 0)
    ky = draw_ky(jax.random.fold_in(key_list[7], 71), 0)
    kt = jnp.clip(jax.random.uniform(key_list[6], (DAYS, DAYS), jnp.float32, 0.25, 1.0), 0.25, 1.0)
    return {"probes": probes, "cells": cells, "fractions": fractions, "counts": counts, "kx": kx, "ky": ky, "kt": kt}


def keys_weights(fraction):
    first = ((-0.5 * fraction + 1.0) * fraction - 0.5) * fraction
    second = (1.5 * fraction - 2.5) * fraction * fraction + 1.0
    third = ((-1.5 * fraction + 2.0) * fraction + 0.5) * fraction
    fourth = (0.5 * fraction - 0.5) * fraction * fraction
    return (first, second, third, fourth)


def reference(probes, cells, fractions, counts, kx, ky, kt):
    points = probes.shape[1]
    slots = jnp.arange(points, dtype=jnp.int32)
    device = slots // PTS_DEV
    live_mask = ((slots % PTS_DEV) // BLOCK < counts.reshape(-1)[device]).astype(jnp.float32)
    row_cell = cells[0]
    col_cell = cells[1]
    day_cell = cells[2]
    weights_x = keys_weights(fractions[0])
    weights_y = [lax.optimization_barrier(w_part.astype(jnp.bfloat16)).astype(jnp.float32) for w_part in keys_weights(fractions[1])]
    weights_t = (1.0 - fractions[2], fractions[2])
    values = probes.astype(jnp.float32) * live_mask[None, :]
    channel = jnp.arange(PROBES, dtype=jnp.int32)
    grid_sum = jnp.zeros((DAYS, PROBES, NX + 3, NY + 3), jnp.float32)
    for step_x in range(4):
        for step_t in range(2):
            timed_values = weights_t[step_t][None, :] * values
            weighted = lax.optimization_barrier((timed_values * weights_x[step_x][None, :]).astype(jnp.bfloat16)).astype(jnp.float32)
            for step_y in range(4):
                grid_sum = grid_sum.at[(day_cell + step_t)[None, :], channel[:, None], (row_cell + step_x)[None, :], (col_cell + step_y)[None, :]].add(weighted * weights_y[step_y][None, :])
    grid_sum = grid_sum[:, :, 1:NX + 1, 1:NY + 1].astype(jnp.bfloat16)
    mixed_x = jnp.einsum("xz,tqzy->tqxy", kx.astype(jnp.float32), grid_sum.astype(jnp.float32), precision=lax.Precision.HIGHEST).astype(jnp.bfloat16)
    crossed = jnp.einsum("yz,tqxz->tqxy", ky.astype(jnp.float32), mixed_x.astype(jnp.float32), precision=lax.Precision.HIGHEST)
    smooth = jnp.einsum("st,tqxy->sqxy", kt, crossed, precision=lax.Precision.HIGHEST).astype(jnp.bfloat16)
    padded = jnp.pad(smooth.astype(jnp.float32), ((0, 0), (0, 0), (1, 2), (1, 2)))
    result = jnp.zeros((PROBES, points), jnp.float32)
    for step_x in range(4):
        inner_sum = jnp.zeros((PROBES, points), jnp.float32)
        for step_t in range(2):
            line_sum = jnp.zeros((PROBES, points), jnp.float32)
            for step_y in range(4):
                picked = padded[day_cell + step_t, :, row_cell + step_x, col_cell + step_y]
                line_sum = line_sum + weights_y[step_y][None, :] * picked.T
            inner_sum = inner_sum + weights_t[step_t][None, :] * line_sum
        result = result + weights_x[step_x][None, :] * inner_sum
    return (result * live_mask[None, :]).astype(jnp.bfloat16)
```

```python
import functools

import jax
import jax.numpy as jnp
from jax import lax
from jax.experimental import pallas as pl
from jax.experimental.pallas import tpu as pltpu
from jax.sharding import PartitionSpec as P

DAYS = 4
PROBES = 8
BLOCK = 128
LANES = 128
RIM = 16
CHUNK = 512
VMEM_BYTES = 48 * 1024 * 1024


def keys_weights(fraction):
    first = ((-0.5 * fraction + 1.0) * fraction - 0.5) * fraction
    second = (1.5 * fraction - 2.5) * fraction * fraction + 1.0
    third = ((-1.5 * fraction + 2.0) * fraction + 0.5) * fraction
    fourth = (0.5 * fraction - 0.5) * fraction * fraction
    return (first, second, third, fourth)


def chosen(delta, weights):
    result = jnp.zeros(delta.shape, weights[0].dtype)
    for k, weight in enumerate(weights):
        result = jnp.where(delta == k, weight, result)
    return result


def distance(cell, rows, first):
    width = cell.shape[1]
    return lax.broadcasted_iota(jnp.int32, (rows, width), 0) + first - cell


def store_columns(ys, cell, fraction, tile_cols):
    weights = [w.astype(jnp.bfloat16).astype(jnp.float32) for w in keys_weights(fraction)]
    ys[0:tile_cols, :] = chosen(distance(cell, tile_cols, 1), weights).astype(jnp.bfloat16)
    row = lax.broadcasted_iota(jnp.int32, (RIM, cell.shape[1]), 0)
    column = jnp.where(row < 2, row + tile_cols, jnp.where(row == 2, -1, -8))
    ys[tile_cols : tile_cols + RIM, :] = chosen(column + 1 - cell, weights).astype(jnp.bfloat16)


def chunks_of(count):
    per = CHUNK // BLOCK
    return (count + per - 1) // per


def scatter_kernel(counts, points, out, total, xs, ys):
    tiles = points.shape[0]
    tile_cols = ys.shape[0] - RIM
    tile_rows = xs.shape[1] - LANES
    used = tile_rows + RIM
    total[...] = jnp.zeros_like(total)
    xs[...] = jnp.zeros_like(xs)

    def tile_step(tile, _):
        lanes = pl.ds(pl.multiple_of(tile * tile_rows, LANES), tile_rows + LANES)

        def chunk_step(number, _):
            part = points[tile, :, pl.ds(pl.multiple_of(number * CHUNK, CHUNK), CHUNK)]
            cell_x = part[0:1].astype(jnp.int32)
            cell_y = part[1:2].astype(jnp.int32)
            day = part[2:3].astype(jnp.int32)
            value = part[7:8]
            store_columns(ys, cell_y, part[5:6], tile_cols)
            early = (1.0 - part[6:7]) * value
            late = part[6:7] * value
            wx = keys_weights(part[4:5])
            z0 = [(early * w).astype(jnp.bfloat16).astype(jnp.float32) for w in wx]
            z1 = [(late * w).astype(jnp.bfloat16).astype(jnp.float32) for w in wx]
            delta = distance(cell_x, used, 0)
            for t in range(DAYS):
                picked = [
                    jnp.where(day == t, a, jnp.where(day == t - 1, b, 0.0)) for a, b in zip(z0, z1)
                ]
                xs[t, 0:used, :] = chosen(delta, picked).astype(jnp.bfloat16)
            for t in range(DAYS):
                total[t, :, lanes] += lax.dot_general(
                    ys[...], xs[t], (((1,), (1,)), ((), ())), preferred_element_type=jnp.float32
                )
            return 0

        lax.fori_loop(0, chunks_of(counts[tile]), chunk_step, 0)
        return 0

    lax.fori_loop(0, tiles, tile_step, 0)
    for t in range(DAYS):
        out[t] = total[t][:, 1 : 1 + out.shape[2]]


def gather_kernel(counts, points, smooth, out, ys):
    tiles = points.shape[0]
    width = smooth.shape[2]
    tile_cols = width - LANES
    tile_rows = (smooth.shape[1] - RIM) // tiles
    used = tile_rows + RIM
    ys[...] = jnp.zeros_like(ys)

    def tile_step(tile, _):
        rows = pl.ds(pl.multiple_of(tile * tile_rows, LANES), used)

        def chunk_step(number, _):
            lanes = pl.ds(pl.multiple_of(number * CHUNK, CHUNK), CHUNK)
            part = points[tile, :, lanes]
            cell_x = part[0:1].astype(jnp.int32)
            cell_y = part[1:2].astype(jnp.int32)
            day = part[2:3].astype(jnp.int32)
            store_columns(ys, cell_y, part[5:6], tile_cols)
            spread_x = chosen(distance(cell_x, used, 0), keys_weights(part[4:5]))
            late = part[6:7]
            result = jnp.zeros((1, CHUNK), jnp.float32)
            for t in range(DAYS):
                line = jnp.dot(
                    smooth[t, rows, :], ys[...], preferred_element_type=jnp.float32
                )
                line = jnp.sum(line * spread_x, axis=0, keepdims=True)
                weight = jnp.where(day == t, 1.0 - late, jnp.where(day == t - 1, late, 0.0))
                result = result + weight * line
            out[tile, :, lanes] = result
            return 0

        lax.fori_loop(0, chunks_of(counts[tile]), chunk_step, 0)
        return 0

    lax.fori_loop(0, tiles, tile_step, 0)


def whole(space=pltpu.VMEM):
    return pl.BlockSpec(memory_space=space)


def body(probes, cells, fractions, counts, kx, ky, kt):
    tile_rows, order_x = kx.shape
    tile_cols, order_y = ky.shape
    points = probes.shape[1]
    tiles_x = lax.axis_size("gx")
    tiles_y = lax.axis_size("gy")
    row_start = lax.axis_index("gx") * tile_rows
    col_start = lax.axis_index("gy") * tile_cols
    live = lax.iota(jnp.int32, points) // BLOCK < counts[0, 0]
    local = jnp.concatenate(
        [
            cells - jnp.stack([row_start, col_start, jnp.int32(0)])[:, None],
            jnp.broadcast_to(counts, (1, points)),
        ],
        axis=0,
    ).astype(jnp.float32)
    local = jnp.concatenate([local, fractions, jnp.zeros((1, points), jnp.float32)], axis=0)
    values = jnp.where(live[None, :], probes, jnp.zeros_like(probes))
    values = lax.all_to_all(values, "gx", split_axis=0, concat_axis=0, tiled=True)
    gathered = lax.all_gather(local, "gx", axis=0, tiled=False)
    all_counts = gathered[:, 3, 0].astype(jnp.int32)
    strip = jnp.concatenate([gathered[:, 0:7], values.astype(jnp.float32)[:, None, :]], axis=1)
    all_kx = lax.all_gather(kx, "gx", axis=0, tiled=True)
    all_ky = lax.all_gather(ky, "gy", axis=0, tiled=True)
    params = pltpu.CompilerParams(vmem_limit_bytes=VMEM_BYTES)
    extended = pl.pallas_call(
        scatter_kernel,
        out_shape=jax.ShapeDtypeStruct((DAYS, tile_cols + RIM, order_x), jnp.float32),
        in_specs=[whole(pltpu.SMEM), whole()],
        out_specs=whole(),
        scratch_shapes=[
            pltpu.VMEM((DAYS, tile_cols + RIM, order_x + LANES), jnp.float32),
            pltpu.VMEM((DAYS, tile_rows + LANES, CHUNK), jnp.bfloat16),
            pltpu.VMEM((tile_cols + RIM, CHUNK), jnp.bfloat16),
        ],
        compiler_params=params,
        name="scatter",
    )(all_counts, strip)
    rim = extended[:, tile_cols : tile_cols + 3]
    forward = [(i, i + 1) for i in range(tiles_y - 1)]
    backward = [(target, source) for source, target in forward]
    low = lax.ppermute(rim[:, 0:2], "gy", forward)
    high = lax.ppermute(rim[:, 2:3], "gy", backward)
    grid_sum = extended[:, :tile_cols]
    grid_sum = grid_sum + jnp.pad(low, ((0, 0), (0, tile_cols - 2), (0, 0)))
    grid_sum = grid_sum + jnp.pad(high, ((0, 0), (tile_cols - 1, 0), (0, 0)))
    grid_sum = grid_sum.astype(jnp.bfloat16)
    last = (((1,), (1,)), ((), ()))
    part_rows = order_x // tiles_y
    mixed_x = jnp.stack(
        [
            lax.dot_general(all_kx, grid_sum[t], last, preferred_element_type=jnp.float32)
            .astype(jnp.bfloat16)
            .reshape(tiles_y, part_rows, tile_cols)
            for t in range(DAYS)
        ],
        axis=1,
    )
    mixed_x = lax.all_to_all(mixed_x, "gy", split_axis=0, concat_axis=0, tiled=True)
    mixed_x = mixed_x.reshape(tiles_y, DAYS * part_rows, tile_cols)
    mixed_x = jnp.concatenate([mixed_x[j] for j in range(tiles_y)], axis=1)
    crossed = lax.dot_general(mixed_x, all_ky, last, preferred_element_type=jnp.float32)
    crossed = crossed.reshape(DAYS, part_rows, order_y)
    smooth = sum(kt[:, t][:, None, None] * crossed[t][None] for t in range(DAYS))
    smooth = jnp.pad(smooth.astype(jnp.bfloat16), ((0, 0), (0, 0), (1, 2)))
    parts = []
    for j in range(tiles_y):
        start = j * tile_cols
        end = start + tile_cols
        piece = jnp.concatenate(
            [smooth[:, :, start + 1 : end + 3], smooth[:, :, start : start + 1]], axis=2
        )
        parts.append(jnp.pad(piece, ((0, 0), (0, 0), (0, LANES - 3))))
    smooth = lax.all_to_all(jnp.stack(parts), "gy", split_axis=0, concat_axis=0, tiled=True)
    smooth = jnp.concatenate([smooth[j] for j in range(tiles_y)], axis=1)
    smooth = jnp.pad(smooth, ((0, 0), (1, RIM - 1), (0, 0)))
    picked = pl.pallas_call(
        gather_kernel,
        out_shape=jax.ShapeDtypeStruct((tiles_x, 1, points), jnp.float32),
        in_specs=[whole(pltpu.SMEM), whole(), whole()],
        out_specs=whole(),
        scratch_shapes=[pltpu.VMEM((tile_cols + LANES, CHUNK), jnp.bfloat16)],
        compiler_params=params,
        name="gather",
    )(all_counts, strip, smooth)
    applied = lax.all_to_all(
        picked[:, 0].astype(jnp.bfloat16), "gx", split_axis=0, concat_axis=0, tiled=True
    )
    return jnp.where(live[None, :], applied, jnp.zeros_like(applied))


def extended_2(block, sides, width):
    for axis, dim in sides:
        count = lax.axis_size(axis)
        forward = [(i, i + 1) for i in range(count - 1)]
        backward = [(target, source) for source, target in forward]
        low = lax.ppermute(
            lax.slice_in_dim(block, block.shape[dim] - width, None, axis=dim), axis, forward
        )
        high = lax.ppermute(lax.slice_in_dim(block, 0, width, axis=dim), axis, backward)
        block = jnp.concatenate([low, block, high], axis=dim)
    return block


def spread(cell_index, weights, extent):
    column = lax.broadcasted_iota(jnp.int32, (cell_index.shape[0], extent), 1)
    result = jnp.zeros((cell_index.shape[0], extent), jnp.float32)
    for offset_k, weight in enumerate(weights):
        result = result + jnp.where(
            column == (cell_index + offset_k)[:, None], weight[:, None], 0.0
        )
    return result


def grid_body(probes, cells, fractions, counts, kx, ky, kt):
    tile_rows = kx.shape[0]
    tile_cols = ky.shape[0]
    channels = DAYS * PROBES
    points = probes.shape[1]
    row_start = lax.axis_index("gx") * tile_rows
    col_start = lax.axis_index("gy") * tile_cols
    weights_x = spread(cells[0] - row_start, keys_weights(fractions[0]), tile_rows + 3)
    weights_y = spread(
        cells[1] - col_start,
        tuple(
            (
                w_part.astype(jnp.bfloat16).astype(jnp.float32)
                for w_part in keys_weights(fractions[1])
            )
        ),
        tile_cols + 3,
    ).astype(jnp.bfloat16)
    weights_t = spread(cells[2], (1.0 - fractions[2], fractions[2]), DAYS)
    live_mask = (lax.iota(jnp.int32, points) // BLOCK < counts[0, 0]).astype(jnp.float32)
    group_size = min(1024, points)
    group_count = points // group_size

    def scatter_group(number, running):
        offset = number * group_size
        x_part = lax.dynamic_slice_in_dim(weights_x, offset, group_size, 0)
        y_part = lax.dynamic_slice_in_dim(weights_y, offset, group_size, 0)
        t_part = lax.dynamic_slice_in_dim(weights_t, offset, group_size, 0)
        mask_part = lax.dynamic_slice_in_dim(live_mask, offset, group_size, 0)
        probe_part = (
            lax.dynamic_slice_in_dim(probes, offset, group_size, 1).astype(jnp.float32)
            * mask_part[None, :]
        )
        timed_values = t_part[:, :, None] * probe_part.T[:, None, :]
        weighted = (timed_values.reshape(group_size, 1, channels) * x_part[:, :, None]).astype(
            jnp.bfloat16
        )
        return running + jnp.einsum(
            "pac,pb->acb", weighted, y_part, preferred_element_type=jnp.float32
        )

    extended = lax.fori_loop(
        0,
        group_count,
        scatter_group,
        jnp.zeros((tile_rows + 3, channels, tile_cols + 3), jnp.float32),
    )
    rim_rows = jnp.concatenate([extended[0:1], extended[tile_rows + 1 : tile_rows + 3]], axis=0)
    received = extended_2(rim_rows, (("gx", 0),), 2)
    core_sum = extended[1 : tile_rows + 1]
    core_sum = core_sum + jnp.pad(received[0:2], ((0, tile_rows - 2), (0, 0), (0, 0)))
    core_sum = core_sum + jnp.pad(received[5:6], ((tile_rows - 1, 0), (0, 0), (0, 0)))
    rim_cols = jnp.concatenate(
        [core_sum[:, :, 0:1], core_sum[:, :, tile_cols + 1 : tile_cols + 3]], axis=2
    )
    received = extended_2(rim_cols, (("gy", 2),), 2)
    grid_sum = core_sum[:, :, 1 : tile_cols + 1]
    grid_sum = grid_sum + jnp.pad(received[:, :, 0:2], ((0, 0), (0, 0), (0, tile_cols - 2)))
    grid_sum = grid_sum + jnp.pad(received[:, :, 5:6], ((0, 0), (0, 0), (tile_cols - 1, 0)))
    grid_sum = grid_sum.astype(jnp.bfloat16)
    whole_kx = lax.all_gather(kx, "gx", axis=0, tiled=True)
    flattened = grid_sum.reshape(tile_rows, channels * tile_cols)
    columns = lax.all_to_all(flattened, "gx", split_axis=1, concat_axis=0, tiled=True)
    product = jnp.dot(whole_kx, columns, preferred_element_type=jnp.float32).astype(jnp.bfloat16)
    mixed_x = lax.all_to_all(product, "gx", split_axis=0, concat_axis=1, tiled=True).reshape(
        tile_rows, channels, tile_cols
    )
    crossed = jnp.einsum(
        "xcn,yn->xcy",
        lax.all_gather(mixed_x, "gy", axis=2, tiled=True),
        ky,
        preferred_element_type=jnp.float32,
    )
    crossed = crossed.reshape(tile_rows, DAYS, PROBES, tile_cols)
    smooth = jnp.einsum("st,xtqy->xsqy", kt, crossed, precision=lax.Precision.HIGHEST)
    smooth = smooth.reshape(tile_rows, channels, tile_cols).astype(jnp.bfloat16)
    padded = extended_2(smooth, (("gx", 0), ("gy", 2)), 2)
    window = padded[1:, :, 1:]

    def gather_group(number, result):
        offset = number * group_size
        x_part = lax.dynamic_slice_in_dim(weights_x, offset, group_size, 0)
        y_part = lax.dynamic_slice_in_dim(weights_y, offset, group_size, 0)
        t_part = lax.dynamic_slice_in_dim(weights_t, offset, group_size, 0)
        mask_part = lax.dynamic_slice_in_dim(live_mask, offset, group_size, 0)
        hidden = jnp.einsum("pb,acb->pac", y_part, window, preferred_element_type=jnp.float32)
        hidden = hidden.reshape(group_size, tile_rows + 3, DAYS, PROBES)
        summed = jnp.einsum(
            "pa,pt,patq->qp", x_part, t_part, hidden, precision=lax.Precision.HIGHEST
        )
        summed = (summed * mask_part[None, :]).astype(jnp.bfloat16)
        return lax.dynamic_update_slice_in_dim(result, summed, offset, 1)

    return lax.fori_loop(0, group_count, gather_group, jnp.zeros((PROBES, points), jnp.bfloat16))


def solution(mesh):
    fits = mesh.shape["gx"] == PROBES and mesh.shape["gy"] == DAYS
    return jax.shard_map(
        body if fits else grid_body,
        mesh=mesh,
        in_specs=(
            P(None, ("gx", "gy")),
            P(None, ("gx", "gy")),
            P(None, ("gx", "gy")),
            P("gx", "gy"),
            P("gx", None),
            P("gy", None),
            P(),
        ),
        out_specs=P(None, ("gx", "gy")),
        check_vma=False,
    )
```

```python
import functools

import jax
import jax.numpy as jnp
from jax import lax
from jax.experimental import pallas as pl
from jax.experimental.pallas import tpu as pltpu
from jax.sharding import PartitionSpec as P

DAYS = 4
PROBES = 8
BLOCK = 128
LANES = 128
RIM = 16
CHUNK = 512
VMEM_BYTES = 48 * 1024 * 1024


def keys_weights(fraction):
    first = ((-0.5 * fraction + 1.0) * fraction - 0.5) * fraction
    second = (1.5 * fraction - 2.5) * fraction * fraction + 1.0
    third = ((-1.5 * fraction + 2.0) * fraction + 0.5) * fraction
    fourth = (0.5 * fraction - 0.5) * fraction * fraction
    return (first, second, third, fourth)


def chosen(delta, weights):
    result = jnp.zeros(delta.shape, weights[0].dtype)
    for k, weight in enumerate(weights):
        result = jnp.where(delta == k, weight, result)
    return result


def distance(cell, rows, first):
    width = cell.shape[1]
    return lax.broadcasted_iota(jnp.int32, (rows, width), 0) + first - cell


def store_columns(ys, cell, fraction, tile_cols):
    weights = [w.astype(jnp.bfloat16).astype(jnp.float32) for w in keys_weights(fraction)]
    ys[0:tile_cols, :] = chosen(distance(cell, tile_cols, 1), weights).astype(jnp.bfloat16)
    row = lax.broadcasted_iota(jnp.int32, (RIM, cell.shape[1]), 0)
    column = jnp.where(row < 2, row + tile_cols, jnp.where(row == RIM - 1, -1, -8))
    ys[tile_cols : tile_cols + RIM, :] = chosen(column + 1 - cell, weights).astype(jnp.bfloat16)


def chunks_of(count):
    per = CHUNK // BLOCK
    return (count + per - 1) // per


def scatter_kernel(counts, points, out, total, xs, ys):
    tiles = points.shape[0]
    tile_cols = ys.shape[0] - RIM
    tile_rows = xs.shape[1] - LANES
    used = tile_rows + RIM
    total[...] = jnp.zeros_like(total)
    xs[...] = jnp.zeros_like(xs)

    def tile_step(tile, _):
        lanes = pl.ds(pl.multiple_of(tile * tile_rows, LANES), tile_rows + LANES)

        def chunk_step(number, _):
            part = points[tile, :, pl.ds(pl.multiple_of(number * CHUNK, CHUNK), CHUNK)]
            cell_x = part[0:1].astype(jnp.int32)
            cell_y = part[1:2].astype(jnp.int32)
            day = part[2:3].astype(jnp.int32)
            value = part[7:8]
            store_columns(ys, cell_y, part[5:6], tile_cols)
            early = (1.0 - part[6:7]) * value
            late = part[6:7] * value
            wx = keys_weights(part[4:5])
            z0 = [(early * w).astype(jnp.bfloat16).astype(jnp.float32) for w in wx]
            z1 = [(late * w).astype(jnp.bfloat16).astype(jnp.float32) for w in wx]
            delta = distance(cell_x, used, 0)
            for t in range(DAYS):
                picked = [
                    jnp.where(day == t, a, jnp.where(day == t - 1, b, 0.0)) for a, b in zip(z0, z1)
                ]
                xs[t, 0:used, :] = chosen(delta, picked).astype(jnp.bfloat16)
            for t in range(DAYS):
                total[t, :, lanes] += lax.dot_general(
                    ys[...], xs[t], (((1,), (1,)), ((), ())), preferred_element_type=jnp.float32
                )
            return 0

        lax.fori_loop(0, chunks_of(counts[tile]), chunk_step, 0)
        return 0

    lax.fori_loop(0, tiles, tile_step, 0)
    for t in range(DAYS):
        out[t] = total[t][:, 1 : 1 + out.shape[2]]


def gather_kernel(counts, points, smooth, out, ys):
    tiles = points.shape[0]
    width = smooth.shape[2]
    tile_cols = width - LANES
    tile_rows = (smooth.shape[1] - 2 * RIM) // tiles
    used = tile_rows + 2 * RIM
    ys[...] = jnp.zeros_like(ys)

    def tile_step(tile, _):
        rows = pl.ds(pl.multiple_of(tile * tile_rows, LANES), used)

        def chunk_step(number, _):
            lanes = pl.ds(pl.multiple_of(number * CHUNK, CHUNK), CHUNK)
            part = points[tile, :, lanes]
            cell_x = part[0:1].astype(jnp.int32)
            cell_y = part[1:2].astype(jnp.int32)
            day = part[2:3].astype(jnp.int32)
            store_columns(ys, cell_y, part[5:6], tile_cols)
            spread_x = chosen(distance(cell_x, used, 1 - RIM), keys_weights(part[4:5]))
            late = part[6:7]
            result = jnp.zeros((1, CHUNK), jnp.float32)
            for t in range(DAYS):
                line = jnp.dot(
                    smooth[t, rows, :], ys[...], preferred_element_type=jnp.float32
                )
                line = jnp.sum(line * spread_x, axis=0, keepdims=True)
                weight = jnp.where(day == t, 1.0 - late, jnp.where(day == t - 1, late, 0.0))
                result = result + weight * line
            out[tile, :, lanes] = result
            return 0

        lax.fori_loop(0, chunks_of(counts[tile]), chunk_step, 0)
        return 0

    lax.fori_loop(0, tiles, tile_step, 0)


def mix_kernel(
    kt, extended, kx, ky, out, rims, mixed_out, mixed_in, total, smooth_out, rim_out, rim_in,
    sem_rims, sem_mixed, sem_smooth, sem_rim,
):
    count = lax.axis_size("gy")
    me = lax.axis_index("gy")
    order = kx.shape[0]
    cols = ky.shape[0] // count
    rows = order // count
    last = (((1,), (1,)), ((), ()))
    peers = [lax.rem(me + p, count) for p in range(count)]

    def remote(src, dst, sems, peer):
        return pltpu.make_async_remote_copy(
            src_ref=src,
            dst_ref=dst,
            send_sem=sems[0],
            recv_sem=sems[1],
            device_id={"gy": peer},
            device_id_type=pl.DeviceIdType.MESH,
        )

    def lanes_of(index):
        return pl.ds(pl.multiple_of(index * cols, LANES), cols)

    def mixed_copy(p, t):
        return remote(
            mixed_out.at[p - 1, t],
            mixed_in.at[t, :, lanes_of(me)],
            (sem_mixed.at[0, p - 1, t], sem_mixed.at[1, p - 1, t]),
            peers[p],
        )

    my_rows = pl.ds(pl.multiple_of(me * rows + RIM, RIM), rows)

    def smooth_copy(p, s):
        return remote(
            smooth_out.at[p - 1, s],
            out.at[s, my_rows, pl.ds(0, cols)],
            (sem_smooth.at[0, p - 1, s], sem_smooth.at[1, p - 1, s]),
            peers[p],
        )

    def rim_copy(p):
        return remote(
            rim_out.at[p - 1],
            rim_in.at[me],
            (sem_rim.at[0, p - 1], sem_rim.at[1, p - 1]),
            peers[p],
        )

    barrier = pltpu.get_barrier_semaphore()
    for p in range(1, count):
        pl.semaphore_signal(
            barrier, inc=1, device_id={"gy": peers[p]}, device_id_type=pl.DeviceIdType.MESH
        )
    pl.semaphore_wait(barrier, count - 1)

    up = remote(
        extended.at[:, pl.ds(cols, 8), :],
        rims.at[0],
        (sem_rims.at[0, 0], sem_rims.at[1, 0]),
        peers[1],
    )
    down = remote(
        extended.at[:, pl.ds(cols + 8, 8), :],
        rims.at[1],
        (sem_rims.at[0, 1], sem_rims.at[1, 1]),
        peers[count - 1],
    )
    up.start()
    down.start()
    out[:, 0:RIM, :] = jnp.zeros((DAYS, RIM, out.shape[2]), out.dtype)
    out[:, order + RIM :, :] = jnp.zeros((DAYS, RIM, out.shape[2]), out.dtype)
    total[...] = jnp.zeros_like(total)
    up.wait()
    down.wait()

    row = lax.broadcasted_iota(jnp.int32, (8, order), 0)
    take_low = jnp.logical_and(row < 2, me > 0)
    take_high = jnp.logical_and(row == 7, me < count - 1)

    def mix_x(t, _):
        grid = jnp.concatenate(
            [
                extended[t, 0:8, :] + jnp.where(take_low, rims[0, t], 0.0),
                extended[t, 8 : cols - 8, :],
                extended[t, cols - 8 : cols, :] + jnp.where(take_high, rims[1, t], 0.0),
            ],
            axis=0,
        ).astype(jnp.bfloat16)
        for p in [*range(1, count), 0]:
            block = lax.dot_general(
                kx[pl.ds(pl.multiple_of(peers[p] * rows, LANES), rows), :],
                grid,
                last,
                preferred_element_type=jnp.float32,
            ).astype(jnp.bfloat16)
            if p:
                mixed_out[p - 1, t] = block
                mixed_copy(p, t).start()
            else:
                mixed_in[t, :, lanes_of(me)] = block
        return 0

    lax.fori_loop(0, DAYS, mix_x, 0)

    def mix_y(t, _):
        for p in range(1, count):
            mixed_copy(p, t).wait()
        for j in range(count):
            part = pl.ds(j * cols, cols)
            crossed = lax.dot_general(
                mixed_in[t], ky[part, :], last, preferred_element_type=jnp.float32
            )
            for s in range(DAYS):
                total[s, :, part] += kt[s, t] * crossed
        return 0

    lax.fori_loop(0, DAYS, mix_y, 0)

    rim_row = lax.broadcasted_iota(jnp.int32, (RIM, rows), 0)

    def send_smooth(s, _):
        for p in [*range(1, count), 0]:
            peer = peers[p]
            block = total[s, :, lanes_of(peer)].astype(jnp.bfloat16)
            after = lax.rem(peer + 1, count) * cols
            before = lax.rem(peer + count - 1, count) * cols + cols - LANES
            after = total[s, :, pl.ds(pl.multiple_of(after, LANES), LANES)].T[0:RIM]
            before = total[s, :, pl.ds(pl.multiple_of(before, LANES), LANES)].T[LANES - RIM :]
            rim = jnp.where(
                jnp.logical_and(rim_row < 2, peer < count - 1),
                after,
                jnp.where(jnp.logical_and(rim_row == RIM - 1, peer > 0), before, 0.0),
            ).astype(jnp.bfloat16)
            if p:
                smooth_out[p - 1, s] = block
                smooth_copy(p, s).start()
                rim_out[p - 1, s] = rim
            else:
                out[s, my_rows, 0:cols] = block
                rim_in[me, s] = rim
        return 0

    lax.fori_loop(0, DAYS, send_smooth, 0)
    for p in range(1, count):
        rim_copy(p).start()
    for p in range(1, count):
        rim_copy(p).wait()
    fill = jnp.zeros((LANES - RIM, rows), jnp.float32)

    def place_rim(s, _):
        for j in range(count):
            rim = jnp.concatenate([rim_in[j, s].astype(jnp.float32), fill], axis=0)
            out[s, pl.ds(j * rows + RIM, rows), cols:] = rim.T.astype(jnp.bfloat16)
        for p in range(1, count):
            smooth_copy(p, s).wait()
        return 0

    lax.fori_loop(0, DAYS, place_rim, 0)


def whole(space=pltpu.VMEM):
    return pl.BlockSpec(memory_space=space)


def body(probes, cells, fractions, counts, kx, ky, kt):
    tile_rows, order_x = kx.shape
    tile_cols, order_y = ky.shape
    points = probes.shape[1]
    tiles_x = lax.axis_size("gx")
    tiles_y = lax.axis_size("gy")
    row_start = lax.axis_index("gx") * tile_rows
    col_start = lax.axis_index("gy") * tile_cols
    live = lax.iota(jnp.int32, points) // BLOCK < counts[0, 0]
    local = jnp.concatenate(
        [
            cells - jnp.stack([row_start, col_start, jnp.int32(0)])[:, None],
            jnp.broadcast_to(counts, (1, points)),
        ],
        axis=0,
    ).astype(jnp.float32)
    local = jnp.concatenate([local, fractions, jnp.zeros((1, points), jnp.float32)], axis=0)
    values = jnp.where(live[None, :], probes, jnp.zeros_like(probes))
    values = lax.all_to_all(values, "gx", split_axis=0, concat_axis=0, tiled=True)
    gathered = lax.all_gather(local, "gx", axis=0, tiled=False)
    all_counts = gathered[:, 3, 0].astype(jnp.int32)
    strip = jnp.concatenate([gathered[:, 0:7], values.astype(jnp.float32)[:, None, :]], axis=1)
    all_kx = lax.all_gather(kx, "gx", axis=0, tiled=True)
    all_ky = lax.all_gather(ky, "gy", axis=0, tiled=True)
    params = pltpu.CompilerParams(vmem_limit_bytes=VMEM_BYTES)
    extended = pl.pallas_call(
        scatter_kernel,
        out_shape=jax.ShapeDtypeStruct((DAYS, tile_cols + RIM, order_x), jnp.float32),
        in_specs=[whole(pltpu.SMEM), whole()],
        out_specs=whole(),
        scratch_shapes=[
            pltpu.VMEM((DAYS, tile_cols + RIM, order_x + LANES), jnp.float32),
            pltpu.VMEM((DAYS, tile_rows + LANES, CHUNK), jnp.bfloat16),
            pltpu.VMEM((tile_cols + RIM, CHUNK), jnp.bfloat16),
        ],
        compiler_params=params,
        name="scatter",
    )(all_counts, strip)
    part_rows = order_x // tiles_y
    smooth = pl.pallas_call(
        mix_kernel,
        out_shape=jax.ShapeDtypeStruct(
            (DAYS, order_x + 2 * RIM, tile_cols + LANES), jnp.bfloat16
        ),
        in_specs=[whole(pltpu.SMEM), whole(), whole(), whole()],
        out_specs=whole(),
        scratch_shapes=[
            pltpu.VMEM((2, DAYS, 8, order_x), jnp.float32),
            pltpu.VMEM((tiles_y - 1, DAYS, part_rows, tile_cols), jnp.bfloat16),
            pltpu.VMEM((DAYS, part_rows, order_y), jnp.bfloat16),
            pltpu.VMEM((DAYS, part_rows, order_y), jnp.float32),
            pltpu.VMEM((tiles_y - 1, DAYS, part_rows, tile_cols), jnp.bfloat16),
            pltpu.VMEM((tiles_y - 1, DAYS, RIM, part_rows), jnp.bfloat16),
            pltpu.VMEM((tiles_y, DAYS, RIM, part_rows), jnp.bfloat16),
            pltpu.SemaphoreType.DMA((2, 2)),
            pltpu.SemaphoreType.DMA((2, tiles_y - 1, DAYS)),
            pltpu.SemaphoreType.DMA((2, tiles_y - 1, DAYS)),
            pltpu.SemaphoreType.DMA((2, tiles_y - 1)),
        ],
        compiler_params=pltpu.CompilerParams(
            vmem_limit_bytes=VMEM_BYTES, collective_id=0, has_side_effects=True
        ),
        name="mix",
    )(kt, extended, all_kx, all_ky)
    picked = pl.pallas_call(
        gather_kernel,
        out_shape=jax.ShapeDtypeStruct((tiles_x, 1, points), jnp.float32),
        in_specs=[whole(pltpu.SMEM), whole(), whole()],
        out_specs=whole(),
        scratch_shapes=[pltpu.VMEM((tile_cols + LANES, CHUNK), jnp.bfloat16)],
        compiler_params=params,
        name="gather",
    )(all_counts, strip, smooth)
    applied = lax.all_to_all(
        picked[:, 0].astype(jnp.bfloat16), "gx", split_axis=0, concat_axis=0, tiled=True
    )
    return jnp.where(live[None, :], applied, jnp.zeros_like(applied))


def extended_2(block, sides, width):
    for axis, dim in sides:
        count = lax.axis_size(axis)
        forward = [(i, i + 1) for i in range(count - 1)]
        backward = [(target, source) for source, target in forward]
        low = lax.ppermute(
            lax.slice_in_dim(block, block.shape[dim] - width, None, axis=dim), axis, forward
        )
        high = lax.ppermute(lax.slice_in_dim(block, 0, width, axis=dim), axis, backward)
        block = jnp.concatenate([low, block, high], axis=dim)
    return block


def spread(cell_index, weights, extent):
    column = lax.broadcasted_iota(jnp.int32, (cell_index.shape[0], extent), 1)
    result = jnp.zeros((cell_index.shape[0], extent), jnp.float32)
    for offset_k, weight in enumerate(weights):
        result = result + jnp.where(
            column == (cell_index + offset_k)[:, None], weight[:, None], 0.0
        )
    return result


def grid_body(probes, cells, fractions, counts, kx, ky, kt):
    tile_rows = kx.shape[0]
    tile_cols = ky.shape[0]
    channels = DAYS * PROBES
    points = probes.shape[1]
    row_start = lax.axis_index("gx") * tile_rows
    col_start = lax.axis_index("gy") * tile_cols
    weights_x = spread(cells[0] - row_start, keys_weights(fractions[0]), tile_rows + 3)
    weights_y = spread(
        cells[1] - col_start,
        tuple(
            (
                w_part.astype(jnp.bfloat16).astype(jnp.float32)
                for w_part in keys_weights(fractions[1])
            )
        ),
        tile_cols + 3,
    ).astype(jnp.bfloat16)
    weights_t = spread(cells[2], (1.0 - fractions[2], fractions[2]), DAYS)
    live_mask = (lax.iota(jnp.int32, points) // BLOCK < counts[0, 0]).astype(jnp.float32)
    group_size = min(1024, points)
    group_count = points // group_size

    def scatter_group(number, running):
        offset = number * group_size
        x_part = lax.dynamic_slice_in_dim(weights_x, offset, group_size, 0)
        y_part = lax.dynamic_slice_in_dim(weights_y, offset, group_size, 0)
        t_part = lax.dynamic_slice_in_dim(weights_t, offset, group_size, 0)
        mask_part = lax.dynamic_slice_in_dim(live_mask, offset, group_size, 0)
        probe_part = (
            lax.dynamic_slice_in_dim(probes, offset, group_size, 1).astype(jnp.float32)
            * mask_part[None, :]
        )
        timed_values = t_part[:, :, None] * probe_part.T[:, None, :]
        weighted = (timed_values.reshape(group_size, 1, channels) * x_part[:, :, None]).astype(
            jnp.bfloat16
        )
        return running + jnp.einsum(
            "pac,pb->acb", weighted, y_part, preferred_element_type=jnp.float32
        )

    extended = lax.fori_loop(
        0,
        group_count,
        scatter_group,
        jnp.zeros((tile_rows + 3, channels, tile_cols + 3), jnp.float32),
    )
    rim_rows = jnp.concatenate([extended[0:1], extended[tile_rows + 1 : tile_rows + 3]], axis=0)
    received = extended_2(rim_rows, (("gx", 0),), 2)
    core_sum = extended[1 : tile_rows + 1]
    core_sum = core_sum + jnp.pad(received[0:2], ((0, tile_rows - 2), (0, 0), (0, 0)))
    core_sum = core_sum + jnp.pad(received[5:6], ((tile_rows - 1, 0), (0, 0), (0, 0)))
    rim_cols = jnp.concatenate(
        [core_sum[:, :, 0:1], core_sum[:, :, tile_cols + 1 : tile_cols + 3]], axis=2
    )
    received = extended_2(rim_cols, (("gy", 2),), 2)
    grid_sum = core_sum[:, :, 1 : tile_cols + 1]
    grid_sum = grid_sum + jnp.pad(received[:, :, 0:2], ((0, 0), (0, 0), (0, tile_cols - 2)))
    grid_sum = grid_sum + jnp.pad(received[:, :, 5:6], ((0, 0), (0, 0), (tile_cols - 1, 0)))
    grid_sum = grid_sum.astype(jnp.bfloat16)
    whole_kx = lax.all_gather(kx, "gx", axis=0, tiled=True)
    flattened = grid_sum.reshape(tile_rows, channels * tile_cols)
    columns = lax.all_to_all(flattened, "gx", split_axis=1, concat_axis=0, tiled=True)
    product = jnp.dot(whole_kx, columns, preferred_element_type=jnp.float32).astype(jnp.bfloat16)
    mixed_x = lax.all_to_all(product, "gx", split_axis=0, concat_axis=1, tiled=True).reshape(
        tile_rows, channels, tile_cols
    )
    crossed = jnp.einsum(
        "xcn,yn->xcy",
        lax.all_gather(mixed_x, "gy", axis=2, tiled=True),
        ky,
        preferred_element_type=jnp.float32,
    )
    crossed = crossed.reshape(tile_rows, DAYS, PROBES, tile_cols)
    smooth = jnp.einsum("st,xtqy->xsqy", kt, crossed, precision=lax.Precision.HIGHEST)
    smooth = smooth.reshape(tile_rows, channels, tile_cols).astype(jnp.bfloat16)
    padded = extended_2(smooth, (("gx", 0), ("gy", 2)), 2)
    window = padded[1:, :, 1:]

    def gather_group(number, result):
        offset = number * group_size
        x_part = lax.dynamic_slice_in_dim(weights_x, offset, group_size, 0)
        y_part = lax.dynamic_slice_in_dim(weights_y, offset, group_size, 0)
        t_part = lax.dynamic_slice_in_dim(weights_t, offset, group_size, 0)
        mask_part = lax.dynamic_slice_in_dim(live_mask, offset, group_size, 0)
        hidden = jnp.einsum("pb,acb->pac", y_part, window, preferred_element_type=jnp.float32)
        hidden = hidden.reshape(group_size, tile_rows + 3, DAYS, PROBES)
        summed = jnp.einsum(
            "pa,pt,patq->qp", x_part, t_part, hidden, precision=lax.Precision.HIGHEST
        )
        summed = (summed * mask_part[None, :]).astype(jnp.bfloat16)
        return lax.dynamic_update_slice_in_dim(result, summed, offset, 1)

    return lax.fori_loop(0, group_count, gather_group, jnp.zeros((PROBES, points), jnp.bfloat16))


def solution(mesh):
    fits = mesh.shape["gx"] == PROBES and mesh.shape["gy"] == DAYS
    return jax.shard_map(
        body if fits else grid_body,
        mesh=mesh,
        in_specs=(
            P(None, ("gx", "gy")),
            P(None, ("gx", "gy")),
            P(None, ("gx", "gy")),
            P("gx", "gy"),
            P("gx", None),
            P("gy", None),
            P(),
        ),
        out_specs=P(None, ("gx", "gy")),
        check_vma=False,
    )
```

```python
import functools

import jax
import jax.numpy as jnp
from jax import lax
from jax.experimental import pallas as pl
from jax.experimental.pallas import tpu as pltpu
from jax.sharding import PartitionSpec as P

DAYS = 4
PROBES = 8
BLOCK = 128
LANES = 128
RIM = 16
CHUNK = 512
VMEM_BYTES = 48 * 1024 * 1024


def keys_weights(fraction):
    first = ((-0.5 * fraction + 1.0) * fraction - 0.5) * fraction
    second = (1.5 * fraction - 2.5) * fraction * fraction + 1.0
    third = ((-1.5 * fraction + 2.0) * fraction + 0.5) * fraction
    fourth = (0.5 * fraction - 0.5) * fraction * fraction
    return (first, second, third, fourth)


def chosen(delta, weights):
    result = jnp.zeros(delta.shape, weights[0].dtype)
    for k, weight in enumerate(weights):
        result = jnp.where(delta == k, weight, result)
    return result


def distance(cell, rows, first):
    width = cell.shape[1]
    return lax.broadcasted_iota(jnp.int32, (rows, width), 0) + first - cell


def packed(row):
    return jnp.broadcast_to(row, (RIM, row.shape[1])).astype(jnp.bfloat16)


def base_of(cell):
    width = cell.shape[1]
    return (lax.broadcasted_iota(jnp.int32, (RIM, width), 0) - cell).astype(jnp.int16)


def store_columns(ys, cell, fraction, tile_cols):
    weights = [packed(w) for w in keys_weights(fraction)]
    base = base_of(cell)
    zero = jnp.zeros(base.shape, jnp.bfloat16)
    for group in range(tile_cols // RIM):
        result = zero
        for k, weight in enumerate(weights):
            result = jnp.where(base == jnp.int16(k - 1 - group * RIM), weight, result)
        ys[group * RIM : (group + 1) * RIM, :] = result
    row = lax.broadcasted_iota(jnp.int32, (RIM, cell.shape[1]), 0)
    column = jnp.where(row < 2, row + tile_cols, jnp.where(row == RIM - 1, -1, -8))
    weights = [w.astype(jnp.bfloat16).astype(jnp.float32) for w in keys_weights(fraction)]
    ys[tile_cols : tile_cols + RIM, :] = chosen(column + 1 - cell, weights).astype(jnp.bfloat16)


def chunks_of(count):
    per = CHUNK // BLOCK
    return (count + per - 1) // per


def scatter_kernel(counts, points, out, total, xs, ys):
    tiles = points.shape[0]
    tile_cols = ys.shape[0] - RIM
    tile_rows = xs.shape[1] - LANES
    used = tile_rows + RIM
    total[...] = jnp.zeros_like(total)
    xs[...] = jnp.zeros_like(xs)

    def tile_step(tile, _):
        lanes = pl.ds(pl.multiple_of(tile * tile_rows, LANES), tile_rows + LANES)

        def chunk_step(number, _):
            part = points[tile, :, pl.ds(pl.multiple_of(number * CHUNK, CHUNK), CHUNK)]
            cell_x = part[0:1].astype(jnp.int32)
            cell_y = part[1:2].astype(jnp.int32)
            day = part[2:3].astype(jnp.int32)
            value = part[7:8]
            store_columns(ys, cell_y, part[5:6], tile_cols)
            early = (1.0 - part[6:7]) * value
            late = part[6:7] * value
            wx = keys_weights(part[4:5])
            picked = [
                [
                    packed(jnp.where(day == t, early * w, jnp.where(day == t - 1, late * w, 0.0)))
                    for w in wx
                ]
                for t in range(DAYS)
            ]
            base = base_of(cell_x)
            zero = jnp.zeros(base.shape, jnp.bfloat16)
            for group in range(used // RIM):
                masks = [base == jnp.int16(k - group * RIM) for k in range(len(wx))]
                for t in range(DAYS):
                    result = zero
                    for mask, weight in zip(masks, picked[t]):
                        result = jnp.where(mask, weight, result)
                    xs[t, group * RIM : (group + 1) * RIM, :] = result
            for t in range(DAYS):
                total[t, :, lanes] += lax.dot_general(
                    ys[...], xs[t], (((1,), (1,)), ((), ())), preferred_element_type=jnp.float32
                )
            return 0

        lax.fori_loop(0, chunks_of(counts[tile]), chunk_step, 0)
        return 0

    lax.fori_loop(0, tiles, tile_step, 0)
    for t in range(DAYS):
        out[t] = total[t][:, 1 : 1 + out.shape[2]]


def gather_kernel(counts, points, smooth, out, ys):
    tiles = points.shape[0]
    width = smooth.shape[2]
    tile_cols = width - LANES
    tile_rows = (smooth.shape[1] - 2 * RIM) // tiles
    used = tile_rows + 2 * RIM
    ys[...] = jnp.zeros_like(ys)

    def tile_step(tile, _):
        rows = pl.ds(pl.multiple_of(tile * tile_rows, LANES), used)

        def chunk_step(number, _):
            lanes = pl.ds(pl.multiple_of(number * CHUNK, CHUNK), CHUNK)
            part = points[tile, :, lanes]
            cell_x = part[0:1].astype(jnp.int32)
            cell_y = part[1:2].astype(jnp.int32)
            day = part[2:3].astype(jnp.int32)
            store_columns(ys, cell_y, part[5:6], tile_cols)
            spread_x = chosen(distance(cell_x, used, 1 - RIM), keys_weights(part[4:5]))
            late = part[6:7]
            result = jnp.zeros((1, CHUNK), jnp.float32)
            for t in range(DAYS):
                line = jnp.dot(
                    smooth[t, rows, :], ys[...], preferred_element_type=jnp.float32
                )
                line = jnp.sum(line * spread_x, axis=0, keepdims=True)
                weight = jnp.where(day == t, 1.0 - late, jnp.where(day == t - 1, late, 0.0))
                result = result + weight * line
            out[tile, :, lanes] = result
            return 0

        lax.fori_loop(0, chunks_of(counts[tile]), chunk_step, 0)
        return 0

    lax.fori_loop(0, tiles, tile_step, 0)


def exchange_kernel(geo, parts, values, geo_all, parts_all, values_all, relay, sem_far, sem_near):
    me = lax.axis_index("gx")
    chips = lax.axis_size("gx") // 2
    chip, core = me // 2, lax.rem(me, 2)
    sibling = chip * 2 + 1 - core

    def remote(src, dst, sems, number, target):
        return pltpu.make_async_remote_copy(
            src_ref=src,
            dst_ref=dst,
            send_sem=sems.at[0, number[0], number[1]],
            recv_sem=sems.at[1, number[0], number[1]],
            device_id={"gx": target},
            device_id_type=pl.DeviceIdType.MESH,
        )

    def far(d):
        there = lax.rem(chip + d, chips) * 2
        target = there + core
        pairs = (
            (geo, geo_all.at[me]),
            (parts, parts_all.at[me]),
            (values.at[target], values_all.at[me]),
            (values.at[there + 1 - core], relay.at[d - 1]),
        )
        return [remote(a, b, sem_far, (d - 1, n), target) for n, (a, b) in enumerate(pairs)]

    def near(d):
        if d == 0:
            pairs = (
                (geo, geo_all.at[me]),
                (parts, parts_all.at[me]),
                (values.at[sibling], values_all.at[me]),
            )
        else:
            source = lax.rem(chip + chips - d, chips) * 2 + core
            pairs = (
                (geo_all.at[source], geo_all.at[source]),
                (parts_all.at[source], parts_all.at[source]),
                (relay.at[d - 1], values_all.at[source]),
            )
        return [remote(a, b, sem_near, (d, n), sibling) for n, (a, b) in enumerate(pairs)]

    partners = [lax.rem(chip + d, chips) * 2 + core for d in range(1, chips)] + [sibling]
    barrier = pltpu.get_barrier_semaphore()
    for partner in partners:
        pl.semaphore_signal(
            barrier, inc=1, device_id={"gx": partner}, device_id_type=pl.DeviceIdType.MESH
        )
    pl.semaphore_wait(barrier, len(partners))

    first = [far(d) for d in range(1, chips)]
    second = [near(d) for d in range(chips)]
    order = [chips // 2, *[d for d in range(1, chips) if d != chips // 2]]
    for d in order:
        for copy in first[d - 1]:
            copy.start()
    for copy in second[0]:
        copy.start()
    geo_all[me] = geo[...]
    parts_all[me] = parts[...]
    values_all[me] = values[me]
    for d in [d for d in range(1, chips) if d != chips // 2] + [chips // 2]:
        for copy in first[d - 1]:
            copy.wait()
        for copy in second[d]:
            copy.start()
    for copies in second:
        for copy in copies:
            copy.wait()


def mix_kernel(
    kt, extended, kx, ky, out, rims, mixed_out, mixed_in, total, smooth_out, rim_out, rim_in,
    sem_rims, sem_mixed, sem_smooth, sem_rim,
):
    count = lax.axis_size("gy")
    me = lax.axis_index("gy")
    order = kx.shape[0]
    cols = ky.shape[0] // count
    rows = order // count
    last = (((1,), (1,)), ((), ()))
    peers = [lax.rem(me + p, count) for p in range(count)]

    def remote(src, dst, sems, peer):
        return pltpu.make_async_remote_copy(
            src_ref=src,
            dst_ref=dst,
            send_sem=sems[0],
            recv_sem=sems[1],
            device_id={"gy": peer},
            device_id_type=pl.DeviceIdType.MESH,
        )

    def lanes_of(index):
        return pl.ds(pl.multiple_of(index * cols, LANES), cols)

    def mixed_copy(p, t):
        return remote(
            mixed_out.at[p - 1, t],
            mixed_in.at[t, :, lanes_of(me)],
            (sem_mixed.at[0, p - 1, t], sem_mixed.at[1, p - 1, t]),
            peers[p],
        )

    my_rows = pl.ds(pl.multiple_of(me * rows + RIM, RIM), rows)

    def smooth_copy(p, s):
        return remote(
            smooth_out.at[p - 1, s],
            out.at[s, my_rows, pl.ds(0, cols)],
            (sem_smooth.at[0, p - 1, s], sem_smooth.at[1, p - 1, s]),
            peers[p],
        )

    def rim_copy(p):
        return remote(
            rim_out.at[p - 1],
            rim_in.at[me],
            (sem_rim.at[0, p - 1], sem_rim.at[1, p - 1]),
            peers[p],
        )

    barrier = pltpu.get_barrier_semaphore()
    for p in range(1, count):
        pl.semaphore_signal(
            barrier, inc=1, device_id={"gy": peers[p]}, device_id_type=pl.DeviceIdType.MESH
        )
    pl.semaphore_wait(barrier, count - 1)

    up = remote(
        extended.at[:, pl.ds(cols, 8), :],
        rims.at[0],
        (sem_rims.at[0, 0], sem_rims.at[1, 0]),
        peers[1],
    )
    down = remote(
        extended.at[:, pl.ds(cols + 8, 8), :],
        rims.at[1],
        (sem_rims.at[0, 1], sem_rims.at[1, 1]),
        peers[count - 1],
    )
    up.start()
    down.start()
    out[:, 0:RIM, :] = jnp.zeros((DAYS, RIM, out.shape[2]), out.dtype)
    out[:, order + RIM :, :] = jnp.zeros((DAYS, RIM, out.shape[2]), out.dtype)
    total[...] = jnp.zeros_like(total)
    up.wait()
    down.wait()

    row = lax.broadcasted_iota(jnp.int32, (8, order), 0)
    take_low = jnp.logical_and(row < 2, me > 0)
    take_high = jnp.logical_and(row == 7, me < count - 1)

    def mix_x(t, _):
        grid = jnp.concatenate(
            [
                extended[t, 0:8, :] + jnp.where(take_low, rims[0, t], 0.0),
                extended[t, 8 : cols - 8, :],
                extended[t, cols - 8 : cols, :] + jnp.where(take_high, rims[1, t], 0.0),
            ],
            axis=0,
        ).astype(jnp.bfloat16)
        for p in [*range(1, count), 0]:
            block = lax.dot_general(
                kx[pl.ds(pl.multiple_of(peers[p] * rows, LANES), rows), :],
                grid,
                last,
                preferred_element_type=jnp.float32,
            ).astype(jnp.bfloat16)
            if p:
                mixed_out[p - 1, t] = block
                mixed_copy(p, t).start()
            else:
                mixed_in[t, :, lanes_of(me)] = block
        return 0

    lax.fori_loop(0, DAYS, mix_x, 0)

    def mix_y(t, _):
        for p in range(1, count):
            mixed_copy(p, t).wait()
        for j in range(count):
            part = pl.ds(j * cols, cols)
            crossed = lax.dot_general(
                mixed_in[t], ky[part, :], last, preferred_element_type=jnp.float32
            )
            for s in range(DAYS):
                total[s, :, part] += kt[s, t] * crossed
        return 0

    lax.fori_loop(0, DAYS, mix_y, 0)

    rim_row = lax.broadcasted_iota(jnp.int32, (RIM, rows), 0)

    def send_smooth(s, _):
        for p in [*range(1, count), 0]:
            peer = peers[p]
            block = total[s, :, lanes_of(peer)].astype(jnp.bfloat16)
            after = lax.rem(peer + 1, count) * cols
            before = lax.rem(peer + count - 1, count) * cols + cols - LANES
            after = total[s, :, pl.ds(pl.multiple_of(after, LANES), LANES)].T[0:RIM]
            before = total[s, :, pl.ds(pl.multiple_of(before, LANES), LANES)].T[LANES - RIM :]
            rim = jnp.where(
                jnp.logical_and(rim_row < 2, peer < count - 1),
                after,
                jnp.where(jnp.logical_and(rim_row == RIM - 1, peer > 0), before, 0.0),
            ).astype(jnp.bfloat16)
            if p:
                smooth_out[p - 1, s] = block
                smooth_copy(p, s).start()
                rim_out[p - 1, s] = rim
            else:
                out[s, my_rows, 0:cols] = block
                rim_in[me, s] = rim
        return 0

    lax.fori_loop(0, DAYS, send_smooth, 0)
    for p in range(1, count):
        rim_copy(p).start()
    for p in range(1, count):
        rim_copy(p).wait()
    fill = jnp.zeros((LANES - RIM, rows), jnp.float32)

    def place_rim(s, _):
        for j in range(count):
            rim = jnp.concatenate([rim_in[j, s].astype(jnp.float32), fill], axis=0)
            out[s, pl.ds(j * rows + RIM, rows), cols:] = rim.T.astype(jnp.bfloat16)
        for p in range(1, count):
            smooth_copy(p, s).wait()
        return 0

    lax.fori_loop(0, DAYS, place_rim, 0)


def whole(space=pltpu.VMEM):
    return pl.BlockSpec(memory_space=space)


def body(probes, cells, fractions, counts, kx, ky, kt):
    tile_rows, order_x = kx.shape
    tile_cols, order_y = ky.shape
    points = probes.shape[1]
    tiles_x = lax.axis_size("gx")
    tiles_y = lax.axis_size("gy")
    row_start = lax.axis_index("gx") * tile_rows
    col_start = lax.axis_index("gy") * tile_cols
    live = lax.iota(jnp.int32, points) // BLOCK < counts[0, 0]
    local = cells - jnp.stack([row_start, col_start, jnp.int32(0)])[:, None]
    high = points // LANES
    geo = jnp.concatenate(
        [local.reshape(3 * high, LANES), jnp.broadcast_to(counts, (RIM, LANES))], axis=0
    ).astype(jnp.bfloat16)
    values = jnp.where(live[None, :], probes, jnp.zeros_like(probes))
    geo, parts, values = pl.pallas_call(
        exchange_kernel,
        out_shape=(
            jax.ShapeDtypeStruct((tiles_x, 3 * high + RIM, LANES), jnp.bfloat16),
            jax.ShapeDtypeStruct((tiles_x, 3 * high, LANES), jnp.float32),
            jax.ShapeDtypeStruct((tiles_x, high, LANES), jnp.bfloat16),
        ),
        in_specs=[whole(), whole(), whole()],
        out_specs=(whole(), whole(), whole()),
        scratch_shapes=[
            pltpu.VMEM((tiles_x // 2 - 1, high, LANES), jnp.bfloat16),
            pltpu.SemaphoreType.DMA((2, tiles_x // 2 - 1, 4)),
            pltpu.SemaphoreType.DMA((2, tiles_x // 2, 3)),
        ],
        compiler_params=pltpu.CompilerParams(
            vmem_limit_bytes=VMEM_BYTES, collective_id=1, has_side_effects=True
        ),
        name="exchange",
    )(geo, fractions.reshape(3 * high, LANES), values.reshape(PROBES, high, LANES))
    all_counts = geo[:, 3 * high, 0].astype(jnp.int32)
    strip = jnp.concatenate(
        [
            geo[:, : 3 * high].astype(jnp.float32).reshape(tiles_x, 3, points),
            jnp.zeros((tiles_x, 1, points), jnp.float32),
            parts.reshape(tiles_x, 3, points),
            values.astype(jnp.float32).reshape(tiles_x, 1, points),
        ],
        axis=1,
    )
    all_kx = lax.all_gather(kx, "gx", axis=0, tiled=True)
    all_ky = lax.all_gather(ky, "gy", axis=0, tiled=True)
    params = pltpu.CompilerParams(vmem_limit_bytes=VMEM_BYTES)
    extended = pl.pallas_call(
        scatter_kernel,
        out_shape=jax.ShapeDtypeStruct((DAYS, tile_cols + RIM, order_x), jnp.float32),
        in_specs=[whole(pltpu.SMEM), whole()],
        out_specs=whole(),
        scratch_shapes=[
            pltpu.VMEM((DAYS, tile_cols + RIM, order_x + LANES), jnp.float32),
            pltpu.VMEM((DAYS, tile_rows + LANES, CHUNK), jnp.bfloat16),
            pltpu.VMEM((tile_cols + RIM, CHUNK), jnp.bfloat16),
        ],
        compiler_params=params,
        name="scatter",
    )(all_counts, strip)
    part_rows = order_x // tiles_y
    smooth = pl.pallas_call(
        mix_kernel,
        out_shape=jax.ShapeDtypeStruct(
            (DAYS, order_x + 2 * RIM, tile_cols + LANES), jnp.bfloat16
        ),
        in_specs=[whole(pltpu.SMEM), whole(), whole(), whole()],
        out_specs=whole(),
        scratch_shapes=[
            pltpu.VMEM((2, DAYS, 8, order_x), jnp.float32),
            pltpu.VMEM((tiles_y - 1, DAYS, part_rows, tile_cols), jnp.bfloat16),
            pltpu.VMEM((DAYS, part_rows, order_y), jnp.bfloat16),
            pltpu.VMEM((DAYS, part_rows, order_y), jnp.float32),
            pltpu.VMEM((tiles_y - 1, DAYS, part_rows, tile_cols), jnp.bfloat16),
            pltpu.VMEM((tiles_y - 1, DAYS, RIM, part_rows), jnp.bfloat16),
            pltpu.VMEM((tiles_y, DAYS, RIM, part_rows), jnp.bfloat16),
            pltpu.SemaphoreType.DMA((2, 2)),
            pltpu.SemaphoreType.DMA((2, tiles_y - 1, DAYS)),
            pltpu.SemaphoreType.DMA((2, tiles_y - 1, DAYS)),
            pltpu.SemaphoreType.DMA((2, tiles_y - 1)),
        ],
        compiler_params=pltpu.CompilerParams(
            vmem_limit_bytes=VMEM_BYTES, collective_id=0, has_side_effects=True
        ),
        name="mix",
    )(kt, extended, all_kx, all_ky)
    picked = pl.pallas_call(
        gather_kernel,
        out_shape=jax.ShapeDtypeStruct((tiles_x, 1, points), jnp.float32),
        in_specs=[whole(pltpu.SMEM), whole(), whole()],
        out_specs=whole(),
        scratch_shapes=[pltpu.VMEM((tile_cols + LANES, CHUNK), jnp.bfloat16)],
        compiler_params=params,
        name="gather",
    )(all_counts, strip, smooth)
    applied = lax.all_to_all(
        picked[:, 0].astype(jnp.bfloat16), "gx", split_axis=0, concat_axis=0, tiled=True
    )
    return jnp.where(live[None, :], applied, jnp.zeros_like(applied))


def extended_2(block, sides, width):
    for axis, dim in sides:
        count = lax.axis_size(axis)
        forward = [(i, i + 1) for i in range(count - 1)]
        backward = [(target, source) for source, target in forward]
        low = lax.ppermute(
            lax.slice_in_dim(block, block.shape[dim] - width, None, axis=dim), axis, forward
        )
        high = lax.ppermute(lax.slice_in_dim(block, 0, width, axis=dim), axis, backward)
        block = jnp.concatenate([low, block, high], axis=dim)
    return block


def spread(cell_index, weights, extent):
    column = lax.broadcasted_iota(jnp.int32, (cell_index.shape[0], extent), 1)
    result = jnp.zeros((cell_index.shape[0], extent), jnp.float32)
    for offset_k, weight in enumerate(weights):
        result = result + jnp.where(
            column == (cell_index + offset_k)[:, None], weight[:, None], 0.0
        )
    return result


def grid_body(probes, cells, fractions, counts, kx, ky, kt):
    tile_rows = kx.shape[0]
    tile_cols = ky.shape[0]
    channels = DAYS * PROBES
    points = probes.shape[1]
    row_start = lax.axis_index("gx") * tile_rows
    col_start = lax.axis_index("gy") * tile_cols
    weights_x = spread(cells[0] - row_start, keys_weights(fractions[0]), tile_rows + 3)
    weights_y = spread(
        cells[1] - col_start,
        tuple(
            (
                w_part.astype(jnp.bfloat16).astype(jnp.float32)
                for w_part in keys_weights(fractions[1])
            )
        ),
        tile_cols + 3,
    ).astype(jnp.bfloat16)
    weights_t = spread(cells[2], (1.0 - fractions[2], fractions[2]), DAYS)
    live_mask = (lax.iota(jnp.int32, points) // BLOCK < counts[0, 0]).astype(jnp.float32)
    group_size = min(1024, points)
    group_count = points // group_size

    def scatter_group(number, running):
        offset = number * group_size
        x_part = lax.dynamic_slice_in_dim(weights_x, offset, group_size, 0)
        y_part = lax.dynamic_slice_in_dim(weights_y, offset, group_size, 0)
        t_part = lax.dynamic_slice_in_dim(weights_t, offset, group_size, 0)
        mask_part = lax.dynamic_slice_in_dim(live_mask, offset, group_size, 0)
        probe_part = (
            lax.dynamic_slice_in_dim(probes, offset, group_size, 1).astype(jnp.float32)
            * mask_part[None, :]
        )
        timed_values = t_part[:, :, None] * probe_part.T[:, None, :]
        weighted = (timed_values.reshape(group_size, 1, channels) * x_part[:, :, None]).astype(
            jnp.bfloat16
        )
        return running + jnp.einsum(
            "pac,pb->acb", weighted, y_part, preferred_element_type=jnp.float32
        )

    extended = lax.fori_loop(
        0,
        group_count,
        scatter_group,
        jnp.zeros((tile_rows + 3, channels, tile_cols + 3), jnp.float32),
    )
    rim_rows = jnp.concatenate([extended[0:1], extended[tile_rows + 1 : tile_rows + 3]], axis=0)
    received = extended_2(rim_rows, (("gx", 0),), 2)
    core_sum = extended[1 : tile_rows + 1]
    core_sum = core_sum + jnp.pad(received[0:2], ((0, tile_rows - 2), (0, 0), (0, 0)))
    core_sum = core_sum + jnp.pad(received[5:6], ((tile_rows - 1, 0), (0, 0), (0, 0)))
    rim_cols = jnp.concatenate(
        [core_sum[:, :, 0:1], core_sum[:, :, tile_cols + 1 : tile_cols + 3]], axis=2
    )
    received = extended_2(rim_cols, (("gy", 2),), 2)
    grid_sum = core_sum[:, :, 1 : tile_cols + 1]
    grid_sum = grid_sum + jnp.pad(received[:, :, 0:2], ((0, 0), (0, 0), (0, tile_cols - 2)))
    grid_sum = grid_sum + jnp.pad(received[:, :, 5:6], ((0, 0), (0, 0), (tile_cols - 1, 0)))
    grid_sum = grid_sum.astype(jnp.bfloat16)
    whole_kx = lax.all_gather(kx, "gx", axis=0, tiled=True)
    flattened = grid_sum.reshape(tile_rows, channels * tile_cols)
    columns = lax.all_to_all(flattened, "gx", split_axis=1, concat_axis=0, tiled=True)
    product = jnp.dot(whole_kx, columns, preferred_element_type=jnp.float32).astype(jnp.bfloat16)
    mixed_x = lax.all_to_all(product, "gx", split_axis=0, concat_axis=1, tiled=True).reshape(
        tile_rows, channels, tile_cols
    )
    crossed = jnp.einsum(
        "xcn,yn->xcy",
        lax.all_gather(mixed_x, "gy", axis=2, tiled=True),
        ky,
        preferred_element_type=jnp.float32,
    )
    crossed = crossed.reshape(tile_rows, DAYS, PROBES, tile_cols)
    smooth = jnp.einsum("st,xtqy->xsqy", kt, crossed, precision=lax.Precision.HIGHEST)
    smooth = smooth.reshape(tile_rows, channels, tile_cols).astype(jnp.bfloat16)
    padded = extended_2(smooth, (("gx", 0), ("gy", 2)), 2)
    window = padded[1:, :, 1:]

    def gather_group(number, result):
        offset = number * group_size
        x_part = lax.dynamic_slice_in_dim(weights_x, offset, group_size, 0)
        y_part = lax.dynamic_slice_in_dim(weights_y, offset, group_size, 0)
        t_part = lax.dynamic_slice_in_dim(weights_t, offset, group_size, 0)
        mask_part = lax.dynamic_slice_in_dim(live_mask, offset, group_size, 0)
        hidden = jnp.einsum("pb,acb->pac", y_part, window, preferred_element_type=jnp.float32)
        hidden = hidden.reshape(group_size, tile_rows + 3, DAYS, PROBES)
        summed = jnp.einsum(
            "pa,pt,patq->qp", x_part, t_part, hidden, precision=lax.Precision.HIGHEST
        )
        summed = (summed * mask_part[None, :]).astype(jnp.bfloat16)
        return lax.dynamic_update_slice_in_dim(result, summed, offset, 1)

    return lax.fori_loop(0, group_count, gather_group, jnp.zeros((PROBES, points), jnp.bfloat16))


def solution(mesh):
    fits = mesh.shape["gx"] == PROBES and mesh.shape["gy"] == DAYS
    return jax.shard_map(
        body if fits else grid_body,
        mesh=mesh,
        in_specs=(
            P(None, ("gx", "gy")),
            P(None, ("gx", "gy")),
            P(None, ("gx", "gy")),
            P("gx", "gy"),
            P("gx", None),
            P("gy", None),
            P(),
        ),
        out_specs=P(None, ("gx", "gy")),
        check_vma=False,
    )
```
